32 devices in a mesh: row: 8 (over z, y), col: 4 (over x, core).
Axes of the slice: x: 2, y: 2, z: 4, core: 2. Of those that a mesh axis runs over, the one named last changes fastest.
Arguments:
- edit_keys: bfloat16 [256, 14336], P('row', 'col'), may hold values from -6.75 to 6.75
- edit_shifts: bfloat16 [256, 4096], P('row', 'col'), may hold values from -6 to 6
- ridge_scale: float32 [1], replicated, may hold values from 0.5 to 2
Outputs:
- panel_a: float32 [14336, 256], P('row')
- panel_b: float32 [14336, 256], P('row')
- trailing: float32 [14336, 14336], P('row', 'col')
- forward: float32 [14336, 4096], P('row', 'col')
The draws below stay inside these ranges and needn't reach their ends.
All inputs are finite; a program needn't handle non-finite values.
Results may differ from the reference program's by a relative error of at most 0.0003.
Values may be sent and summed in bfloat16 or wider, within the bound.
No kernel may reach another device: no remote copies, remote signals or barrier semaphores. Data moves between devices by JAX's collectives and lax.ppermute only.
A program may use at most 128 MiB of HBM per device.

```python
import math
import jax
import jax.numpy as jnp
from jax import lax

UNITS = 14336
OUT_WIDTH = 4096
KEY_ROWS = 256
PANEL = 256
N_COL = 4


def draw_edit_keys(key, part):
    draw_one = jax.random.fold_in(jax.random.fold_in(key, 11), 0)
    draw_two = jax.random.fold_in(jax.random.fold_in(key, 11), 1)
    draw_three = jax.random.fold_in(jax.random.fold_in(key, 11), 2)
    draw_five = jax.random.fold_in(jax.random.fold_in(key, 11), 4)
    draw_six = jax.random.fold_in(jax.random.fold_in(key, 11), 5)
    draw_seven = jax.random.fold_in(jax.random.fold_in(key, 11), 6)
    trend_rows = 3.0 ** (0.5 * jnp.arange(KEY_ROWS, dtype=jnp.float32) / KEY_ROWS)
    trend_units = 3.0 ** (0.5 * jnp.arange(UNITS, dtype=jnp.float32) / UNITS)
    unit_ids = jnp.arange(UNITS, dtype=jnp.int32)
    start_b = UNITS // N_COL
    loud_units = (unit_ids < PANEL) | (unit_ids >= start_b) & (unit_ids < start_b + PANEL)
    shared_rows = jnp.clip(jax.random.normal(draw_five, (KEY_ROWS, 1), jnp.float32), -2.5, 2.5)
    signs = jnp.where(jax.random.normal(draw_seven, (1, UNITS), jnp.float32) < 0.0, -1.0, 1.0)
    unit_weights = jax.random.uniform(draw_six, (1, UNITS), jnp.float32, 0.6, 1.3) * signs
    noise = jnp.clip(jax.random.normal(draw_one, (KEY_ROWS, UNITS), jnp.float32), -4.0, 4.0)
    quiet_values = noise
    low_end = 0.3
    loud_values = jnp.clip(shared_rows * unit_weights + 0.35 * noise, -4.0, 4.0)
    base_values = jnp.where(loud_units[None, :], loud_values, 0.25 * quiet_values)
    row_scale = jnp.exp(jax.random.uniform(draw_two, (KEY_ROWS,), jnp.float32, math.log(low_end), math.log(3.0)))
    unit_scale = jnp.exp(jax.random.uniform(draw_three, (UNITS,), jnp.float32, math.log(low_end), math.log(3.0)))
    scaled = base_values * (row_scale * trend_rows)[:, None] * (unit_scale * trend_units)[None, :]
    return (scaled / math.sqrt(KEY_ROWS)).astype(jnp.bfloat16)


def steps_of(rng, shape, cuts, smallest, top_value):
    factor_of, own = 1.0, jax.random.fold_in(rng, 6)
    for position, blocks in cuts:
        heights = jnp.exp(jax.random.uniform(jax.random.fold_in(own, position), (blocks,), jnp.float32, smallest / len(cuts), top_value / len(cuts)))
        factor_of = factor_of * jnp.repeat(heights, shape[position] // blocks).reshape([-1 if axis == position else 1 for axis in range(len(shape))])
    return factor_of


def centred(rng, extent, width, most, shards=(), held_as=jnp.bfloat16):
    entries = width * jax.random.normal(rng, extent, jnp.float32)
    if shards:
        entries = entries * steps_of(rng, extent, shards, -0.22, 0.18)
    return jnp.clip(entries, -most, most).astype(held_as)


def setup_inputs(seed: int = 0) -> dict:
    seeds = jax.random.split(jax.random.key(seed), 4)
    return {
        "edit_keys": draw_edit_keys(jax.random.fold_in(seeds[3], 71), 0),
        "edit_shifts": centred(seeds[1], (KEY_ROWS, OUT_WIDTH), 1.0, 6.0, ((0, 8), (1, 4))),
        "ridge_scale": jnp.clip(jnp.exp(jax.random.uniform(seeds[2], (1,), jnp.float32, math.log(0.5), math.log(2.0))), 0.5, 2.0),
    }


def reference(edit_keys, edit_shifts, ridge_scale):
    widened = edit_keys.astype(jnp.float32)
    amount = ridge_scale[0] * jnp.sum(widened * widened) / UNITS
    gram = jnp.dot(edit_keys.T.astype(jnp.float32), edit_keys.astype(jnp.float32), preferred_element_type=jnp.float32)
    diagonal_ids = jnp.arange(UNITS, dtype=jnp.int32)
    gram = gram.at[diagonal_ids, diagonal_ids].add(amount)
    rhs_full = jnp.dot(edit_keys.T.astype(jnp.float32), edit_shifts.astype(jnp.float32), preferred_element_type=jnp.float32)
    start_b = UNITS // N_COL
    lower_a = jnp.linalg.cholesky(gram[:PANEL, :PANEL])
    panel_a = jax.scipy.linalg.solve_triangular(lower_a, gram[:, :PANEL].T, lower=True).T
    panel_a = panel_a.at[:PANEL].set(lower_a)
    solved_a = jax.scipy.linalg.solve_triangular(lower_a, rhs_full[:PANEL], lower=True)
    column_b = gram[:, start_b:start_b + PANEL] - jnp.dot(panel_a, panel_a[start_b:start_b + PANEL].T, precision=lax.Precision.HIGHEST)
    lower_b = jnp.linalg.cholesky(column_b[start_b:start_b + PANEL])
    panel_b = jax.scipy.linalg.solve_triangular(lower_b, column_b.T, lower=True).T
    panel_b = panel_b.at[:PANEL].set(0.0).at[start_b:start_b + PANEL].set(lower_b)
    rhs_one = rhs_full - jnp.dot(panel_a, solved_a, precision=lax.Precision.HIGHEST)
    solved_b = jax.scipy.linalg.solve_triangular(lower_b, rhs_one[start_b:start_b + PANEL], lower=True)
    rhs_two = rhs_one - jnp.dot(panel_b, solved_b, precision=lax.Precision.HIGHEST)
    both_panels = jnp.concatenate([panel_a, panel_b], axis=1)
    trailing = gram - jnp.dot(both_panels, both_panels.T, precision=lax.Precision.HIGHEST)
    dropped = (diagonal_ids < PANEL) | (diagonal_ids >= start_b) & (diagonal_ids < start_b + PANEL)
    trailing = jnp.where(dropped[:, None] | dropped[None, :], 0.0, trailing)
    forward = rhs_two.at[:PANEL].set(solved_a).at[start_b:start_b + PANEL].set(solved_b)
    return (panel_a, panel_b, trailing, forward)
```

```python
import functools
import jax
import jax.numpy as jnp
from jax import lax
from jax.experimental import pallas as pl
from jax.experimental.pallas import tpu as pltpu
from jax.sharding import PartitionSpec as P

PANEL = 256
CHUNK = 128
GROUP = 64
WIDTH = 256
SLOTS = 3
EXACT = lax.Precision.HIGHEST
VMEM = pl.BlockSpec(memory_space=pltpu.VMEM)
SMEM = pl.BlockSpec(memory_space=pltpu.SMEM)
ANY = pl.BlockSpec(memory_space=pl.ANY)


def iota(shape, dim):
    return lax.broadcasted_iota(jnp.int32, shape, dim)


def product(left_side, right_side, left_dim, right_dim, precision=None):
    return lax.dot_general(
        left_side,
        right_side,
        (((left_dim,), (right_dim,)), ((), ())),
        precision=precision,
        preferred_element_type=jnp.float32,
    )


def split_three(value):
    high = value.astype(jnp.bfloat16)
    rest = value - high.astype(jnp.float32)
    middle = rest.astype(jnp.bfloat16)
    low = (rest - middle.astype(jnp.float32)).astype(jnp.bfloat16)
    return high, middle, low


def store_sums(out_ref, top, sums):
    high, middle, low = (term.astype(jnp.float32) for term in split_three(sums))
    upper = jnp.concatenate([high, middle], axis=1)
    lower = jnp.concatenate([low, jnp.zeros_like(low)], axis=1)
    out_ref[top : top + 16, 0:256] = jnp.concatenate([upper, lower], axis=0).astype(jnp.bfloat16)


def load_sums(rows):
    wide = rows.astype(jnp.float32)
    return wide[0:8, 0:128] + wide[0:8, 128:256] + wide[8:16, 0:128]


def pack_kernel(keys_ref, out_ref):
    rows, units = keys_ref.shape
    out_ref[0:rows, :] = keys_ref[:, 0:PANEL]
    sums = jnp.zeros((8, 128), jnp.float32)
    for lane in range(0, units, 128):
        wide = keys_ref[:, lane : lane + 128].astype(jnp.float32)
        squares = wide * wide
        for top in range(0, rows, 8):
            sums = sums + squares[top : top + 8]
    store_sums(out_ref, rows, sums)


def merge_kernel(gathered_ref, out_ref):
    cols, rows, _ = gathered_ref.shape
    rows = rows - 16
    out_ref[...] = jnp.zeros(out_ref.shape, out_ref.dtype)
    out_ref[0:rows, 0:PANEL] = gathered_ref[0, 0:rows, :]
    out_ref[0:rows, PANEL : 2 * PANEL] = gathered_ref[1, 0:rows, :]
    sums = jnp.zeros((8, 128), jnp.float32)
    for col in range(cols):
        sums = sums + load_sums(gathered_ref[col, rows : rows + 16, :])
    store_sums(out_ref, rows, sums)


def factor_group(tiles, base):
    lane = iota((8, 128), 1)
    sub = iota((8, 128), 0)
    diagonals = []
    for top in range(len(tiles)):
        live = range(top, len(tiles))
        first = base + 8 * top
        columns = [
            {at: jnp.broadcast_to(tiles[at][:, first + q : first + q + 1], (8, 128)) for at in live}
            for q in range(8)
        ]
        scale = jnp.zeros((8, 128), jnp.float32)
        pivots = jnp.zeros((8, 128), jnp.float32)
        for q in range(8):
            column = columns[q]
            pivot = jnp.broadcast_to(column[top][q : q + 1, :], (8, 128))
            inverse = 1.0 / pivot
            for k in range(q + 1, 8):
                factor = jnp.broadcast_to(column[top][k : k + 1, :], (8, 128)) * inverse
                for at in live:
                    columns[k][at] = columns[k][at] - column[at] * factor
            row = jnp.broadcast_to(tiles[top][q : q + 1, :], (8, 128))
            row = jnp.where(lane == first + q, 1.0, row)
            scaled = row * inverse
            for at in live:
                kept = jnp.where(lane == first + q, 0.0, tiles[at])
                new = kept - column[at] * scaled
                if at == top:
                    new = jnp.where(sub < q, tiles[at], jnp.where(sub == q, row, new))
                tiles[at] = new
            scale = jnp.where(sub == q, lax.rsqrt(pivot), scale)
            pivots = jnp.where(sub == q, pivot, pivots)
        tiles[top] = tiles[top] * scale
        diagonals.append(pivots * scale)
    return tiles, diagonals


def factor_chunk(work):
    lane = iota((CHUNK, CHUNK), 1)
    row = iota((CHUNK, CHUNK), 0)
    diagonals = []
    for base in range(0, CHUNK, GROUP):
        rest = base + GROUP
        tiles = [work[top : top + 8, :] for top in range(base, rest, 8)]
        tiles, found = factor_group(tiles, base)
        diagonals += found
        done = jnp.concatenate(tiles, axis=0)
        work[base:rest, :] = done
        if rest < CHUNK:
            group_lane = lane[base:rest]
            upper = (group_lane > row[base:rest]) & (group_lane < rest)
            update = product(done, jnp.where(upper, 0.0, done), 0, 0, EXACT)[rest:]
            later_lane = lane[rest:]
            own = (later_lane >= base) & (later_lane < rest)
            work[rest:, :] = jnp.where(own, 0.0, work[rest:, :]) - update
    both = work[...]
    diagonal = jnp.concatenate(diagonals, axis=0)
    inverse = jnp.where(lane <= row, both, 0.0)
    factor = jnp.where(lane > row, both, jnp.where(lane == row, diagonal, 0.0))
    return inverse, factor


def eliminate_kernel(
    total_units, ids_ref, ridge_ref, packed_ref, amount_ref, lower_ref, vectors_ref, middle_ref, keys, work
):
    shards = packed_ref.shape[0]
    rows = packed_ref.shape[1] - 16
    own = ids_ref[0]
    sums = jnp.zeros((8, 128), jnp.float32)
    for shard in range(shards):
        keys[shard * rows : (shard + 1) * rows, :] = packed_ref[own ^ shard, 0:rows, :]
        sums = sums + load_sums(packed_ref[shard, rows : rows + 16, 0:256])
    total = jnp.sum(jnp.sum(sums, axis=0, keepdims=True), axis=1, keepdims=True)
    amount = total * ridge_ref[0] / total_units
    amount_ref[...] = jnp.broadcast_to(amount, amount_ref.shape)
    held = keys[...]
    depth = held.shape[0]
    chunks = 2 * PANEL // CHUNK
    gram = product(held, held, 0, 0)
    flipped = held.astype(jnp.float32).T
    square = (CHUNK, CHUNK)
    ridge = jnp.where(iota(square, 0) == iota(square, 1), jnp.broadcast_to(amount, square), 0.0)
    solved = []
    factors = []
    middle = jnp.where(iota((depth, depth), 0) == iota((depth, depth), 1), 1.0, 0.0)
    for chunk in range(chunks):
        low, high = chunk * CHUNK, (chunk + 1) * CHUNK
        block = gram[low:high, low:high] + ridge
        for row in solved:
            block = block - product(row[:, low:high], row[:, low:high], 0, 0, EXACT)
        work[chunk] = block
        later = flipped[low:high, :]
        if high < gram.shape[1]:
            later = jnp.concatenate([gram[low:high, high:], later], axis=1)
        for row in solved:
            later = later - product(row[:, low:high], row[:, high:], 0, 0, EXACT)
        inverse, factor = factor_chunk(work.at[chunk])
        later = product(inverse, later, 1, 0, EXACT)
        solved.append(jnp.concatenate([jnp.zeros((CHUNK, high), jnp.float32), later], axis=1))
        factors.append(factor)
        vector = later[:, -depth:]
        vectors_ref[:, low:high] = vector.T
        middle = middle - product(vector, vector, 0, 0, EXACT)
    middle_ref[...] = middle
    for panel in range(2):
        first = 2 * panel
        left = first * CHUNK
        side = solved[first][:, left + CHUNK : left + 2 * CHUNK]
        upper = jnp.concatenate([factors[first], side], axis=1)
        under = jnp.concatenate([jnp.zeros(square, jnp.float32), factors[first + 1]], axis=1)
        lower_ref[panel] = jnp.concatenate([upper, under], axis=0).T


def tile_kernel(
    sizes,
    ids_ref,
    amount_ref,
    lower_ref,
    vectors_ref,
    middle_ref,
    row_keys_ref,
    right_ref,
    panel_a_ref,
    panel_b_ref,
    trailing_ref,
    forward_ref,
    left,
    right,
    terms,
    out,
    sems,
):
    band, col_units, steps = sizes
    step = pl.program_id(0)
    slot = lax.rem(step, SLOTS)
    row_index = ids_ref[0]
    col_index = ids_ref[1]
    depth, row_units = row_keys_ref.shape
    col_steps = col_units // WIDTH
    block = step - 2

    @pl.when(step == 0)
    def _():
        flipped = row_keys_ref[...].astype(jnp.float32).T.astype(jnp.bfloat16)
        left[:, 0:depth] = flipped
        left[:, depth : 2 * depth] = flipped
        for place, term in enumerate(split_three(middle_ref[...])):
            terms[place] = term

    def put_right(value):
        high = value.astype(jnp.bfloat16)
        right[0:depth, :] = high
        right[depth : 2 * depth, :] = (value - high.astype(jnp.float32)).astype(jnp.bfloat16)

    @pl.when(step < 2)
    def _():
        put_right(vectors_ref[:, pl.ds(pl.multiple_of(step * PANEL, PANEL), PANEL)])

    @pl.when(step >= 2)
    def _():
        keys = right_ref[...]
        value = product(terms[2], keys, 1, 0) + product(terms[1], keys, 1, 0)
        put_right(value + product(terms[0], keys, 1, 0))

    def copy_out(target):
        return pltpu.make_async_copy(out.at[slot], target, sems.at[slot])

    @pl.when(step >= SLOTS)
    def _():
        copy_out(panel_a_ref).wait()

    out[slot] = product(left[...], right[...], 1, 0)

    in_a = row_index == 0
    in_b = row_index == band
    zeros = jnp.zeros((PANEL, WIDTH), jnp.float32)

    @pl.when((step == 0) & in_a)
    def _():
        out[slot, 0:PANEL, :] = lower_ref[0]

    @pl.when((step == 1) & in_a)
    def _():
        out[slot, 0:PANEL, :] = zeros

    @pl.when((step == 1) & in_b)
    def _():
        out[slot, 0:PANEL, :] = lower_ref[1]

    is_trailing = (block >= 0) & (block < col_steps)
    is_forward = block >= col_steps
    apart = col_index * col_units + block * WIDTH - row_index * row_units

    @pl.when(is_trailing & (apart > -WIDTH) & (apart < row_units))
    def _():
        top = pl.multiple_of(jnp.clip(apart, 0, row_units - WIDTH), 64)
        square = (WIDTH, WIDTH)
        near = iota(square, 0) + (top - apart) == iota(square, 1)
        amount = jnp.broadcast_to(amount_ref[0:1, 0:1], square)
        held = out[slot, pl.ds(top, WIDTH), :]
        out[slot, pl.ds(top, WIDTH), :] = held + jnp.where(near, amount, 0.0)

    @pl.when(is_trailing & (in_a | in_b))
    def _():
        out[slot, 0:PANEL, :] = zeros

    @pl.when((block == 0) & (col_index < 2))
    def _():
        out[slot] = jnp.zeros((row_units, WIDTH), jnp.float32)

    @pl.when(is_forward & (in_a | in_b))
    def _():
        first = pl.multiple_of(jnp.where(in_a, 0, PANEL), PANEL)
        vectors = vectors_ref[:, pl.ds(first, PANEL)].T
        high, mid, low = split_three(vectors)
        shifts = right_ref[...]
        value = product(low, shifts, 1, 0) + product(mid, shifts, 1, 0)
        out[slot, 0:PANEL, :] = value + product(high, shifts, 1, 0)

    @pl.when(step == 0)
    def _():
        copy_out(panel_a_ref).start()

    @pl.when(step == 1)
    def _():
        copy_out(panel_b_ref).start()

    @pl.when(is_trailing)
    def _():
        at = pl.multiple_of(block * WIDTH, WIDTH)
        copy_out(trailing_ref.at[:, pl.ds(at, WIDTH)]).start()

    @pl.when(is_forward)
    def _():
        at = pl.multiple_of((block - col_steps) * WIDTH, WIDTH)
        copy_out(forward_ref.at[:, pl.ds(at, WIDTH)]).start()

    @pl.when(step == steps - 1)
    def _():
        for place in range(SLOTS):
            pltpu.make_async_copy(out.at[place], panel_a_ref, sems.at[place]).wait()


def double_up(block, axis, count):
    step = 1
    while step < count:
        pairs = [(place, place ^ step) for place in range(count)]
        block = jnp.concatenate([block, lax.ppermute(block, axis, pairs)], axis=0)
        step *= 2
    return block


def on_device(edit_keys, edit_shifts, ridge_scale):
    row_count = lax.axis_size("row")
    col_count = lax.axis_size("col")
    row_index = lax.axis_index("row")
    col_index = lax.axis_index("col")
    rows, col_units = edit_keys.shape
    shift_cols = edit_shifts.shape[1]
    depth = rows * row_count
    total_units = col_units * col_count
    row_units = total_units // row_count
    band = row_count // col_count
    ids = jnp.stack([row_index, col_index]).astype(jnp.int32)

    rights = lax.all_gather(
        jnp.concatenate([edit_keys, edit_shifts], axis=1), "row", axis=0, tiled=True
    )

    pieces = []
    for turn in range(band):
        part = (row_index + turn) % band
        piece = lax.dynamic_slice_in_dim(edit_keys, part * row_units, row_units, 1)
        pairs = []
        for row in range(row_count):
            for col in range(col_count):
                target = (col * band + (row + turn) % band) * col_count + row // band
                pairs.append((row * col_count + col, target))
        pieces.append(lax.ppermute(piece, ("row", "col"), pairs))

    packed = pl.pallas_call(
        pack_kernel,
        out_shape=jax.ShapeDtypeStruct((rows + 16, PANEL), jnp.bfloat16),
        in_specs=[VMEM],
        out_specs=VMEM,
    )(edit_keys)
    merged = pl.pallas_call(
        merge_kernel,
        out_shape=jax.ShapeDtypeStruct((rows + 16, 2 * PANEL), jnp.bfloat16),
        in_specs=[VMEM],
        out_specs=VMEM,
    )(lax.all_gather(packed, "col", axis=0))
    everyone = double_up(merged[None], "row", row_count)

    amount, lower, vectors, middle = pl.pallas_call(
        functools.partial(eliminate_kernel, total_units),
        out_shape=(
            jax.ShapeDtypeStruct((8, 128), jnp.float32),
            jax.ShapeDtypeStruct((2, PANEL, PANEL), jnp.float32),
            jax.ShapeDtypeStruct((depth, 2 * PANEL), jnp.float32),
            jax.ShapeDtypeStruct((depth, depth), jnp.float32),
        ),
        in_specs=[SMEM, SMEM, VMEM],
        out_specs=(VMEM, VMEM, VMEM, VMEM),
        scratch_shapes=[
            pltpu.VMEM((depth, 2 * PANEL), jnp.bfloat16),
            pltpu.VMEM((2 * PANEL // CHUNK, CHUNK, CHUNK), jnp.float32),
        ],
        compiler_params=pltpu.CompilerParams(vmem_limit_bytes=32 * 2**20),
        cost_estimate=pl.CostEstimate(flops=2 * 10**10, bytes_accessed=10**6, transcendentals=0),
    )(ids, ridge_scale, everyone)

    part = row_index % band
    stacked = jnp.stack(pieces)
    ordered = [
        lax.dynamic_index_in_dim(stacked, (part - place) % band, 0, keepdims=False)
        for place in range(band)
    ]
    row_keys = lax.all_gather(jnp.concatenate(ordered, axis=0), "col", axis=0, tiled=True)

    col_steps = col_units // WIDTH
    steps = 2 + col_steps + shift_cols // WIDTH
    return tuple(
        pl.pallas_call(
            functools.partial(tile_kernel, (band, col_units, steps)),
            grid=(steps,),
            out_shape=(
                jax.ShapeDtypeStruct((row_units, PANEL), jnp.float32),
                jax.ShapeDtypeStruct((row_units, PANEL), jnp.float32),
                jax.ShapeDtypeStruct((row_units, col_units), jnp.float32),
                jax.ShapeDtypeStruct((row_units, shift_cols), jnp.float32),
            ),
            in_specs=[
                SMEM,
                VMEM,
                VMEM,
                VMEM,
                VMEM,
                VMEM,
                pl.BlockSpec((depth, WIDTH), lambda step: (0, jnp.maximum(step - 2, 0))),
            ],
            out_specs=(ANY, ANY, ANY, ANY),
            scratch_shapes=[
                pltpu.VMEM((row_units, 2 * depth), jnp.bfloat16),
                pltpu.VMEM((2 * depth, WIDTH), jnp.bfloat16),
                pltpu.VMEM((3, depth, depth), jnp.bfloat16),
                pltpu.VMEM((SLOTS, row_units, WIDTH), jnp.float32),
                pltpu.SemaphoreType.DMA((SLOTS,)),
            ],
            compiler_params=pltpu.CompilerParams(vmem_limit_bytes=40 * 2**20),
            cost_estimate=pl.CostEstimate(
                flops=10**10, bytes_accessed=4 * 10**7, transcendentals=0
            ),
        )(ids, amount, lower, vectors, middle, row_keys, rights)
    )


def solution(mesh):
    return jax.shard_map(
        on_device,
        mesh=mesh,
        in_specs=(P("row", "col"), P("row", "col"), P()),
        out_specs=(P("row", None), P("row", None), P("row", "col"), P("row", "col")),
        check_vma=False,
    )
```

```python
import functools
import jax
import jax.numpy as jnp
from jax import lax
from jax.experimental import pallas as pl
from jax.experimental.pallas import tpu as pltpu
from jax.sharding import PartitionSpec as P

PANEL = 256
CHUNK = 128
GROUP = 64
SLOTS = 3
EXACT = lax.Precision.HIGHEST
VMEM = pl.BlockSpec(memory_space=pltpu.VMEM)
SMEM = pl.BlockSpec(memory_space=pltpu.SMEM)
ANY = pl.BlockSpec(memory_space=pl.ANY)


def iota(shape, dim):
    return lax.broadcasted_iota(jnp.int32, shape, dim)


def product(left_side, right_side, left_dim, right_dim, precision=None):
    return lax.dot_general(
        left_side,
        right_side,
        (((left_dim,), (right_dim,)), ((), ())),
        precision=precision,
        preferred_element_type=jnp.float32,
    )


def split_three(value):
    high = value.astype(jnp.bfloat16)
    rest = value - high.astype(jnp.float32)
    middle = rest.astype(jnp.bfloat16)
    low = (rest - middle.astype(jnp.float32)).astype(jnp.bfloat16)
    return high, middle, low


def store_sums(out_ref, top, sums):
    high, middle, low = (term.astype(jnp.float32) for term in split_three(sums))
    upper = jnp.concatenate([high, middle], axis=1)
    lower = jnp.concatenate([low, jnp.zeros_like(low)], axis=1)
    out_ref[top : top + 16, 0:256] = jnp.concatenate([upper, lower], axis=0).astype(jnp.bfloat16)


def load_sums(rows):
    wide = rows.astype(jnp.float32)
    return wide[0:8, 0:128] + wide[0:8, 128:256] + wide[8:16, 0:128]


def pack_kernel(band, keys_ref, shifts_ref, packed_ref, rights_ref, *piece_refs):
    rows, units = keys_ref.shape
    row_units = units // band
    packed_ref[0:rows, :] = keys_ref[:, 0:PANEL]
    sums = jnp.zeros((8, 128), jnp.float32)
    for lane in range(0, units, 128):
        wide = keys_ref[:, lane : lane + 128].astype(jnp.float32)
        squares = wide * wide
        for top in range(0, rows, 8):
            sums = sums + squares[top : top + 8]
    store_sums(packed_ref, rows, sums)
    rights_ref[:, 0:units] = keys_ref[...]
    rights_ref[:, units:] = shifts_ref[...]
    for turn in range(band):
        for part in range(band):

            @pl.when(lax.rem(lax.axis_index("row") + turn, band) == part)
            def _():
                piece_refs[turn][...] = keys_ref[:, part * row_units : (part + 1) * row_units]


def add_kernel(one_ref, other_ref, out_ref):
    store_sums(out_ref, 0, load_sums(one_ref[...]) + load_sums(other_ref[...]))


def factor_group(tiles, base):
    lane = iota((8, 128), 1)
    sub = iota((8, 128), 0)
    diagonals = []
    for top in range(len(tiles)):
        live = range(top, len(tiles))
        first = base + 8 * top
        columns = [
            {at: jnp.broadcast_to(tiles[at][:, first + q : first + q + 1], (8, 128)) for at in live}
            for q in range(8)
        ]
        scale = jnp.zeros((8, 128), jnp.float32)
        pivots = jnp.zeros((8, 128), jnp.float32)
        for q in range(8):
            column = columns[q]
            pivot = jnp.broadcast_to(column[top][q : q + 1, :], (8, 128))
            inverse = 1.0 / pivot
            for k in range(q + 1, 8):
                factor = jnp.broadcast_to(column[top][k : k + 1, :], (8, 128)) * inverse
                for at in live:
                    columns[k][at] = columns[k][at] - column[at] * factor
            row = jnp.broadcast_to(tiles[top][q : q + 1, :], (8, 128))
            row = jnp.where(lane == first + q, 1.0, row)
            scaled = row * inverse
            for at in live:
                kept = jnp.where(lane == first + q, 0.0, tiles[at])
                new = kept - column[at] * scaled
                if at == top:
                    new = jnp.where(sub < q, tiles[at], jnp.where(sub == q, row, new))
                tiles[at] = new
            scale = jnp.where(sub == q, lax.rsqrt(pivot), scale)
            pivots = jnp.where(sub == q, pivot, pivots)
        tiles[top] = tiles[top] * scale
        diagonals.append(pivots * scale)
    return tiles, diagonals


def factor_chunk(work):
    lane = iota((CHUNK, CHUNK), 1)
    row = iota((CHUNK, CHUNK), 0)
    diagonals = []
    for base in range(0, CHUNK, GROUP):
        rest = base + GROUP
        tiles = [work[top : top + 8, :] for top in range(base, rest, 8)]
        tiles, found = factor_group(tiles, base)
        diagonals += found
        done = jnp.concatenate(tiles, axis=0)
        work[base:rest, :] = done
        if rest < CHUNK:
            group_lane = lane[base:rest]
            upper = (group_lane > row[base:rest]) & (group_lane < rest)
            update = product(done, jnp.where(upper, 0.0, done), 0, 0, EXACT)[rest:]
            later_lane = lane[rest:]
            own = (later_lane >= base) & (later_lane < rest)
            work[rest:, :] = jnp.where(own, 0.0, work[rest:, :]) - update
    both = work[...]
    diagonal = jnp.concatenate(diagonals, axis=0)
    inverse = jnp.where(lane <= row, both, 0.0)
    factor = jnp.where(lane > row, both, jnp.where(lane == row, diagonal, 0.0))
    return inverse, factor


def snake_place(row, row_count, band):
    lines = row_count // band
    line, place = row // band, lax.rem(row, band)
    back = lines - 1 - line
    inner = jnp.where(lax.rem(back, 2) == 0, place - 1, band - 1 - place)
    return jnp.where(place == 0, line, lines + back * (band - 1) + inner)


def eliminate_panel(rows, carried, ridge, work):
    solved = []
    factors = []
    for chunk, row in enumerate(rows):
        low, high = chunk * CHUNK, (chunk + 1) * CHUNK
        block = row[:, low:high] + ridge
        for done in carried + solved:
            block = block - product(done[:, low:high], done[:, low:high], 0, 0, EXACT)
        work[chunk] = block
        later = row[:, high:]
        for done in carried + solved:
            later = later - product(done[:, low:high], done[:, high:], 0, 0, EXACT)
        inverse, factor = factor_chunk(work.at[chunk])
        later = product(inverse, later, 1, 0, EXACT)
        solved.append(jnp.concatenate([jnp.zeros((CHUNK, high), jnp.float32), later], axis=1))
        factors.append(factor)
    square = jnp.zeros((CHUNK, CHUNK), jnp.float32)
    upper = jnp.concatenate([factors[0], solved[0][:, CHUNK : 2 * CHUNK]], axis=1)
    under = jnp.concatenate([square, factors[1]], axis=1)
    return solved, jnp.concatenate([upper, under], axis=0).T


def put_vectors(solved, middle, vectors_ref, heads_ref):
    depth = vectors_ref.shape[0]
    for chunk, row in enumerate(solved):
        low, high = chunk * CHUNK, (chunk + 1) * CHUNK
        vector = row[:, -depth:]
        vectors_ref[:, low:high] = vector.T
        first, second, _ = split_three(vector)
        heads_ref[low:high, 0:depth] = first
        heads_ref[low:high, depth : 2 * depth] = second
        middle = middle - product(vector, vector, 0, 0, EXACT)
    return middle


def ridge_of(amount):
    square = (CHUNK, CHUNK)
    near = iota(square, 0) == iota(square, 1)
    return jnp.where(near, jnp.broadcast_to(amount, square), 0.0)


def first_kernel(
    total_units,
    masks,
    band,
    ridge_ref,
    near_ref,
    far_ref,
    near_mate_ref,
    far_mate_ref,
    amount_ref,
    lower_ref,
    vectors_ref,
    heads_ref,
    carried_ref,
    middle_ref,
    keys_ref,
    staged,
    keys,
    work,
):
    half = near_ref.shape[0]
    rows = near_ref.shape[1] - 32
    row_index = lax.axis_index("row")
    parity = lax.rem(lax.axis_index("col"), 2)
    sums = jnp.zeros((8, 128), jnp.float32)
    for panel, pair in ((parity, (near_ref, far_ref)), (1 - parity, (near_mate_ref, far_mate_ref))):
        for place, source in enumerate(pair):
            for shard in range(half):
                at = snake_place(row_index ^ (masks[shard] + place), 2 * half, band)
                staged[panel, at] = source[shard, 0:rows, :]
                sums = sums + load_sums(source[shard, rows : rows + 16, :])
                sums = sums + load_sums(source[shard, rows + 16 : rows + 32, :])
    for shard in range(2 * half):
        for panel in range(2):
            top, lane = shard * rows, panel * PANEL
            keys[top : top + rows, lane : lane + PANEL] = staged[panel, shard]
    total = jnp.sum(jnp.sum(sums, axis=0, keepdims=True), axis=1, keepdims=True)
    amount = total * ridge_ref[0] / total_units
    amount_ref[...] = jnp.broadcast_to(amount, amount_ref.shape)
    held = keys[...]
    depth = held.shape[0]
    keys_ref[...] = held[:, PANEL:]
    gram = product(held[:, :PANEL], held, 0, 0)
    whole = jnp.concatenate([gram, held[:, :PANEL].astype(jnp.float32).T], axis=1)
    chunks = [whole[low : low + CHUNK] for low in range(0, PANEL, CHUNK)]
    solved, lower = eliminate_panel(chunks, [], ridge_of(amount), work)
    lower_ref[...] = lower
    for chunk, row in enumerate(solved):
        carried_ref[chunk] = row[:, PANEL:]
    middle = jnp.where(iota((depth, depth), 0) == iota((depth, depth), 1), 1.0, 0.0)
    middle_ref[...] = put_vectors(solved, middle, vectors_ref, heads_ref)


def second_kernel(
    amount_ref,
    carried_ref,
    middle_ref,
    keys_ref,
    lower_ref,
    vectors_ref,
    heads_ref,
    terms_ref,
    work,
):
    held = keys_ref[...]
    gram = product(held, held, 0, 0)
    whole = jnp.concatenate([gram, held.astype(jnp.float32).T], axis=1)
    chunks = [whole[low : low + CHUNK] for low in range(0, PANEL, CHUNK)]
    carried = [carried_ref[chunk] for chunk in range(PANEL // CHUNK)]
    solved, lower = eliminate_panel(chunks, carried, ridge_of(amount_ref[0:1, 0:1]), work)
    lower_ref[...] = lower
    middle = put_vectors(solved, middle_ref[...], vectors_ref, heads_ref)
    for place, term in enumerate(split_three(middle)):
        terms_ref[place] = term


def tile_kernel(
    sizes,
    amount_ref,
    terms_ref,
    heads_a_ref,
    heads_b_ref,
    vectors_a_ref,
    vectors_b_ref,
    lower_a_ref,
    lower_b_ref,
    rights_ref,
    *refs,
):
    band, col_units = sizes
    row_refs, refs = refs[:-11], refs[-11:]
    panel_a_ref, panel_b_ref, trailing_ref, forward_ref, *refs = refs
    blocks, right, out, staged, left, block_sems, out_sems = refs
    count, depth, width = blocks.shape
    row_units = left.shape[0]
    col_count = col_units // width
    row_index = lax.axis_index("row")
    col_index = lax.axis_index("col")
    in_a = row_index == 0
    in_b = row_index == band
    loads = [
        pltpu.make_async_copy(
            rights_ref.at[:, step * width : (step + 1) * width], blocks.at[step], block_sems.at[step]
        )
        for step in range(count)
    ]
    for load in loads:
        load.start()
    row_count, rows = staged.shape[0:2]
    part = lax.rem(row_index, band)
    for mask, source in enumerate(row_refs):
        for turn in range(band):
            row = (col_index ^ mask) * band + lax.rem(part - turn + band, band)
            staged[snake_place(row, row_count, band)] = source[turn]
    held = jnp.concatenate([staged[shard] for shard in range(row_count)], axis=0)
    flipped = held.astype(jnp.float32).T.astype(jnp.bfloat16)
    left[:, 0:depth] = flipped
    left[:, depth:] = flipped

    def put_right(step):
        if step < count:
            loads[step].wait()
            block = blocks[step]
            value = product(terms_ref[2], block, 1, 0) + product(terms_ref[1], block, 1, 0)
            value = value + product(terms_ref[0], block, 1, 0)
        else:
            first = (step - count) * width
            parts = (vectors_a_ref, vectors_b_ref)[first // PANEL : (first + width) // PANEL]
            value = jnp.concatenate([ref[...] for ref in parts], axis=1)
        high = value.astype(jnp.bfloat16)
        right[step % 2, 0:depth, :] = high
        right[step % 2, depth:, :] = (value - high.astype(jnp.float32)).astype(jnp.bfloat16)

    def copies(step):
        slot = step % SLOTS
        if step < count:
            target, at = trailing_ref, step * width
            if step >= col_count:
                target, at = forward_ref, (step - col_count) * width
            target = target.at[:, at : at + width]
            return [pltpu.make_async_copy(out.at[slot], target, out_sems.at[slot, 0])]
        first = (step - count) * width
        return [
            pltpu.make_async_copy(
                out.at[slot, :, lane : lane + PANEL],
                (panel_a_ref, panel_b_ref)[(first + lane) // PANEL],
                out_sems.at[slot, lane // PANEL],
            )
            for lane in range(0, width, PANEL)
        ]

    def finish_trailing(step, slot):
        apart = col_index * col_units + step * width - row_index * row_units

        amount = jnp.broadcast_to(amount_ref[0:1, 0:1], (64, 128))

        def add_ridge(piece, carry):
            top = pl.multiple_of(piece * 64, 64)
            lane = pl.multiple_of((top - apart) // 128 * 128, 128)
            near = iota((64, 128), 0) + (top - apart - lane) == iota((64, 128), 1)
            held = out[slot, pl.ds(top, 64), pl.ds(lane, 128)]
            out[slot, pl.ds(top, 64), pl.ds(lane, 128)] = held + jnp.where(near, amount, 0.0)
            return carry

        first = jnp.clip(apart, 0, row_units) // 64
        lax.fori_loop(first, jnp.clip(apart + width, 0, row_units) // 64, add_ridge, 0)

        @pl.when(in_a | in_b)
        def _():
            out[slot, 0:PANEL, :] = jnp.zeros((PANEL, width), jnp.float32)

        if step == 0:

            @pl.when(col_index < 2)
            def _():
                out[slot, :, 0:PANEL] = jnp.zeros((row_units, PANEL), jnp.float32)

    def finish_forward(step, slot):
        for here, heads in ((in_a, heads_a_ref), (in_b, heads_b_ref)):

            @pl.when(here)
            def _():
                block = blocks[step]
                out[slot, 0:PANEL, :] = product(heads[:, 0:depth], block, 1, 0) + product(
                    heads[:, depth:], block, 1, 0
                )

    def finish_panels(step, slot):
        for lane in range(0, width, PANEL):
            panel = ((step - count) * width + lane) // PANEL

            @pl.when(in_a)
            def _():
                block = jnp.zeros((PANEL, PANEL), jnp.float32)
                out[slot, 0:PANEL, lane : lane + PANEL] = block if panel else lower_a_ref[...]

            if panel:

                @pl.when(in_b)
                def _():
                    out[slot, 0:PANEL, lane : lane + PANEL] = lower_b_ref[...]

    steps = count + 2 * PANEL // width
    put_right(0)
    for step in range(steps):
        slot = step % SLOTS
        if step >= SLOTS:
            for copy in copies(step - SLOTS):
                copy.wait()
        if step + 1 < steps:
            put_right(step + 1)
        out[slot] = product(left[...], right[step % 2], 1, 0)
        if step < col_count:
            finish_trailing(step, slot)
        elif step < count:
            finish_forward(step, slot)
        else:
            finish_panels(step, slot)
        for copy in copies(step):
            copy.start()
    for step in range(steps - SLOTS, steps):
        for copy in copies(step):
            copy.wait()


def snake(row_count, band):
    lines = row_count // band
    order = [line * band for line in range(lines)]
    for line in reversed(range(lines)):
        places = [line * band + place for place in range(1, band)]
        order += places if (lines - 1 - line) % 2 == 0 else places[::-1]
    return order


def exchange(block, axis, count, step):
    return lax.ppermute(block, axis, [(place, place ^ step) for place in range(count)])


def on_device(edit_keys, edit_shifts, ridge_scale):
    row_count = lax.axis_size("row")
    col_count = lax.axis_size("col")
    rows, col_units = edit_keys.shape
    shift_cols = edit_shifts.shape[1]
    depth = rows * row_count
    total_units = col_units * col_count
    row_units = total_units // row_count
    band = row_count // col_count

    packed, shares, *pieces = pl.pallas_call(
        functools.partial(pack_kernel, band),
        out_shape=(
            jax.ShapeDtypeStruct((rows + 16, PANEL), jnp.bfloat16),
            jax.ShapeDtypeStruct((rows, col_units + shift_cols), jnp.bfloat16),
        )
        + (jax.ShapeDtypeStruct((rows, row_units), jnp.bfloat16),) * band,
        in_specs=[VMEM, VMEM],
        out_specs=(VMEM,) * (2 + band),
    )(edit_keys, edit_shifts)
    moved = []
    for turn in range(band):
        pairs = []
        for row in range(row_count):
            for col in range(col_count):
                target = (col * band + (row + turn) % band) * col_count + row // band
                pairs.append((row * col_count + col, target))
        moved.append(lax.ppermute(pieces[turn], ("row", "col"), pairs))
    near, sums = packed[:rows], packed[rows:]
    bit = col_count // 2
    while bit > 1:
        other = exchange(packed, "col", col_count, bit)
        low = (lax.axis_index("col") // bit) % 2 == 0
        near = jnp.where(low, packed[:rows], other[:rows])
        sums = [packed[rows:], other[rows:]]
        bit //= 2
        if bit > 1:
            sums = pl.pallas_call(
                add_kernel,
                out_shape=jax.ShapeDtypeStruct((16, PANEL), jnp.bfloat16),
                in_specs=[VMEM, VMEM],
                out_specs=VMEM,
            )(*sums)
            packed = jnp.concatenate([near, sums], axis=0)
    near = jnp.concatenate([near] + sums, axis=0)[None]
    order = snake(row_count, band)
    rights = lax.all_gather(shares, "row", axis=0, tiled=True, axis_index_groups=[order])
    masks = [0]
    bit = row_count // 2
    while bit > 1:
        near = jnp.concatenate([near, exchange(near, "row", row_count, bit)], axis=0)
        masks += [held + bit for held in masks]
        bit //= 2
    far = exchange(near, "row", row_count, 1)
    near_mate = exchange(near, "col", col_count, 1)
    far_mate = exchange(far, "col", col_count, 1)

    part = functools.partial(jax.ShapeDtypeStruct, dtype=jnp.float32)
    part_low = functools.partial(jax.ShapeDtypeStruct, dtype=jnp.bfloat16)
    cost = pl.CostEstimate(flops=10**10, bytes_accessed=10**6, transcendentals=0)
    amount, lower_a, vectors_a, heads_a, carried, middle, keys_b = pl.pallas_call(
        functools.partial(first_kernel, total_units, masks, band),
        out_shape=(
            part((8, 128)),
            part((PANEL, PANEL)),
            part((depth, PANEL)),
            part_low((PANEL, 2 * depth)),
            part((PANEL // CHUNK, CHUNK, PANEL + depth)),
            part((depth, depth)),
            part_low((depth, PANEL)),
        ),
        in_specs=[SMEM] + [VMEM] * 4,
        out_specs=(VMEM,) * 7,
        scratch_shapes=[
            pltpu.VMEM((2, row_count, rows, PANEL), jnp.bfloat16),
            pltpu.VMEM((depth, 2 * PANEL), jnp.bfloat16),
            pltpu.VMEM((PANEL // CHUNK, CHUNK, CHUNK), jnp.float32),
        ],
        compiler_params=pltpu.CompilerParams(vmem_limit_bytes=32 * 2**20),
        cost_estimate=cost,
    )(ridge_scale, near, far, near_mate, far_mate)
    moved, amount = lax.optimization_barrier((moved, amount))
    row_keys = [jnp.stack(moved)]
    for mask in range(1, col_count):
        row_keys.append(exchange(row_keys[0], "col", col_count, mask))
    lower_b, vectors_b, heads_b, terms = pl.pallas_call(
        second_kernel,
        out_shape=(
            part((PANEL, PANEL)),
            part((depth, PANEL)),
            part_low((PANEL, 2 * depth)),
            part_low((3, depth, depth)),
        ),
        in_specs=[VMEM] * 4,
        out_specs=(VMEM,) * 4,
        scratch_shapes=[
            pltpu.VMEM((PANEL // CHUNK, CHUNK, CHUNK), jnp.float32),
        ],
        compiler_params=pltpu.CompilerParams(vmem_limit_bytes=32 * 2**20),
        cost_estimate=cost,
    )(amount, carried, middle, keys_b)

    width = 2 * PANEL
    if col_units % width or shift_cols % width:
        width = PANEL
    count = (col_units + shift_cols) // width
    return tuple(
        pl.pallas_call(
            functools.partial(tile_kernel, (band, col_units)),
            out_shape=(
                jax.ShapeDtypeStruct((row_units, PANEL), jnp.float32),
                jax.ShapeDtypeStruct((row_units, PANEL), jnp.float32),
                jax.ShapeDtypeStruct((row_units, col_units), jnp.float32),
                jax.ShapeDtypeStruct((row_units, shift_cols), jnp.float32),
            ),
            in_specs=[VMEM] * 8 + [ANY] + [VMEM] * col_count,
            out_specs=(ANY, ANY, ANY, ANY),
            scratch_shapes=[
                pltpu.VMEM((count, depth, width), jnp.bfloat16),
                pltpu.VMEM((2, 2 * depth, width), jnp.bfloat16),
                pltpu.VMEM((SLOTS, row_units, width), jnp.float32),
                pltpu.VMEM((row_count, rows, row_units), jnp.bfloat16),
                pltpu.VMEM((row_units, 2 * depth), jnp.bfloat16),
                pltpu.SemaphoreType.DMA((count,)),
                pltpu.SemaphoreType.DMA((SLOTS, 2)),
            ],
            compiler_params=pltpu.CompilerParams(vmem_limit_bytes=40 * 2**20),
            cost_estimate=pl.CostEstimate(
                flops=10**10, bytes_accessed=4 * 10**7, transcendentals=0
            ),
        )(
            amount,
            terms,
            heads_a,
            heads_b,
            vectors_a,
            vectors_b,
            lower_a,
            lower_b,
            rights,
            *row_keys,
        )
    )


def solution(mesh):
    return jax.shard_map(
        on_device,
        mesh=mesh,
        in_specs=(P("row", "col"), P("row", "col"), P()),
        out_specs=(P("row", None), P("row", None), P("row", "col"), P("row", "col")),
        check_vma=False,
    )
```

```python
import functools
import jax
import jax.numpy as jnp
from jax import lax
from jax.experimental import pallas as pl
from jax.experimental.pallas import tpu as pltpu
from jax.sharding import PartitionSpec as P

PANEL = 256
CHUNK = 128
GROUP = 32
SPAN = 16
SLOTS = 3
EXACT = lax.Precision.HIGHEST
VMEM = pl.BlockSpec(memory_space=pltpu.VMEM)
SMEM = pl.BlockSpec(memory_space=pltpu.SMEM)
ANY = pl.BlockSpec(memory_space=pl.ANY)


def iota(shape, dim):
    return lax.broadcasted_iota(jnp.int32, shape, dim)


def product(left_side, right_side, left_dim, right_dim, precision=None):
    return lax.dot_general(
        left_side,
        right_side,
        (((left_dim,), (right_dim,)), ((), ())),
        precision=precision,
        preferred_element_type=jnp.float32,
    )


def split_three(value):
    high = value.astype(jnp.bfloat16)
    rest = value - high.astype(jnp.float32)
    middle = rest.astype(jnp.bfloat16)
    low = (rest - middle.astype(jnp.float32)).astype(jnp.bfloat16)
    return high, middle, low


def store_sums(out_ref, top, sums):
    high, middle, low = (term.astype(jnp.float32) for term in split_three(sums))
    upper = jnp.concatenate([high, middle], axis=1)
    lower = jnp.concatenate([low, jnp.zeros_like(low)], axis=1)
    out_ref[top : top + 16, 0:256] = jnp.concatenate([upper, lower], axis=0).astype(jnp.bfloat16)


def load_sums(rows):
    wide = rows.astype(jnp.float32)
    return wide[0:8, 0:128] + wide[0:8, 128:256] + wide[8:16, 0:128]


def pack_kernel(band, keys_ref, shifts_ref, packed_ref, rights_ref, *piece_refs):
    rows, units = keys_ref.shape
    row_units = units // band
    packed_ref[0:rows, :] = keys_ref[:, 0:PANEL]
    sums = jnp.zeros((8, 128), jnp.float32)
    for lane in range(0, units, 128):
        wide = keys_ref[:, lane : lane + 128].astype(jnp.float32)
        squares = wide * wide
        for top in range(0, rows, 8):
            sums = sums + squares[top : top + 8]
    store_sums(packed_ref, rows, sums)
    rights_ref[:, 0:units] = keys_ref[...]
    rights_ref[:, units:] = shifts_ref[...]
    for turn in range(band):
        for part in range(band):

            @pl.when(lax.rem(lax.axis_index("row") + turn, band) == part)
            def _():
                piece_refs[turn][...] = keys_ref[:, part * row_units : (part + 1) * row_units]


def add_kernel(one_ref, other_ref, out_ref):
    store_sums(out_ref, 0, load_sums(one_ref[...]) + load_sums(other_ref[...]))


def factor_group(tiles, base):
    lane = iota((8, 128), 1)
    sub = iota((8, 128), 0)
    diagonals = []
    for start in range(0, len(tiles), SPAN // 8):
        columns = [
            {
                at: jnp.broadcast_to(tiles[at][:, lane_of : lane_of + 1], (8, 128))
                for at in range((lane_of - base) // 8, len(tiles))
            }
            for lane_of in range(base + 8 * start, base + 8 * start + SPAN)
        ]
        for q in range(SPAN):
            top, own = start + q // 8, q % 8
            first = base + 8 * start + q
            live = range(top, len(tiles))
            column = columns[q]
            pivot = jnp.broadcast_to(column[top][own : own + 1, :], (8, 128))
            inverse = 1.0 / pivot
            for k in range(q + 1, SPAN):
                near = start + k // 8
                factor = jnp.broadcast_to(column[near][k % 8 : k % 8 + 1, :], (8, 128)) * inverse
                for at in range(near, len(tiles)):
                    columns[k][at] = columns[k][at] - column[at] * factor
            row = jnp.broadcast_to(tiles[top][own : own + 1, :], (8, 128))
            row = jnp.where(lane == first, 1.0, row)
            scaled = row * inverse
            for at in live:
                kept = jnp.where(lane == first, 0.0, tiles[at])
                new = kept - column[at] * scaled
                if at == top:
                    new = jnp.where(sub < own, tiles[at], jnp.where(sub == own, row, new))
                tiles[at] = new
            if own == 0:
                scale = jnp.zeros((8, 128), jnp.float32)
                pivots = jnp.zeros((8, 128), jnp.float32)
            scale = jnp.where(sub == own, lax.rsqrt(pivot), scale)
            pivots = jnp.where(sub == own, pivot, pivots)
            if own == 7:
                tiles[top] = tiles[top] * scale
                diagonals.append(pivots * scale)
    return tiles, diagonals


def factor_chunk(work):
    lane = iota((CHUNK, CHUNK), 1)
    row = iota((CHUNK, CHUNK), 0)
    diagonals = []
    for base in range(0, CHUNK, GROUP):
        rest = base + GROUP
        tiles = [work[top : top + 8, :] for top in range(base, rest, 8)]
        tiles, found = factor_group(tiles, base)
        diagonals += found
        done = jnp.concatenate(tiles, axis=0)
        work[base:rest, :] = done
        if rest < CHUNK:
            group_lane = lane[base:rest]
            upper = (group_lane > row[base:rest]) & (group_lane < rest)
            update = product(done, jnp.where(upper, 0.0, done), 0, 0, EXACT)[rest:]
            later_lane = lane[rest:]
            own = (later_lane >= base) & (later_lane < rest)
            work[rest:, :] = jnp.where(own, 0.0, work[rest:, :]) - update
    both = work[...]
    diagonal = jnp.concatenate(diagonals, axis=0)
    inverse = jnp.where(lane <= row, both, 0.0)
    factor = jnp.where(lane > row, both, jnp.where(lane == row, diagonal, 0.0))
    return inverse, factor


def snake_place(row, row_count, band):
    lines = row_count // band
    line, place = row // band, lax.rem(row, band)
    back = lines - 1 - line
    inner = jnp.where(lax.rem(back, 2) == 0, place - 1, band - 1 - place)
    return jnp.where(place == 0, line, lines + back * (band - 1) + inner)


def eliminate_panel(rows, carried, ridge, work):
    solved = []
    factors = []
    for chunk, row in enumerate(rows):
        low, high = chunk * CHUNK, (chunk + 1) * CHUNK
        block = row[:, low:high] + ridge
        for done in carried + solved:
            block = block - product(done[:, low:high], done[:, low:high], 0, 0, EXACT)
        work[chunk] = block
        later = row[:, high:]
        for done in carried + solved:
            later = later - product(done[:, low:high], done[:, high:], 0, 0, EXACT)
        inverse, factor = factor_chunk(work.at[chunk])
        later = product(inverse, later, 1, 0, EXACT)
        solved.append(jnp.concatenate([jnp.zeros((CHUNK, high), jnp.float32), later], axis=1))
        factors.append(factor)
    square = jnp.zeros((CHUNK, CHUNK), jnp.float32)
    upper = jnp.concatenate([factors[0], solved[0][:, CHUNK : 2 * CHUNK]], axis=1)
    under = jnp.concatenate([square, factors[1]], axis=1)
    return solved, jnp.concatenate([upper, under], axis=0).T


def put_vectors(solved, middle, vectors_ref, heads_ref):
    depth = vectors_ref.shape[0]
    for chunk, row in enumerate(solved):
        low, high = chunk * CHUNK, (chunk + 1) * CHUNK
        vector = row[:, -depth:]
        vectors_ref[:, low:high] = vector.T
        first, second, _ = split_three(vector)
        heads_ref[low:high, 0:depth] = first
        heads_ref[low:high, depth : 2 * depth] = second
        middle = middle - product(vector, vector, 0, 0, EXACT)
    return middle


def ridge_of(amount):
    square = (CHUNK, CHUNK)
    near = iota(square, 0) == iota(square, 1)
    return jnp.where(near, jnp.broadcast_to(amount, square), 0.0)


def first_kernel(
    total_units,
    masks,
    band,
    ridge_ref,
    near_ref,
    far_ref,
    near_mate_ref,
    far_mate_ref,
    amount_ref,
    lower_ref,
    vectors_ref,
    heads_ref,
    carried_ref,
    middle_ref,
    keys_ref,
    staged,
    keys,
    work,
):
    half = near_ref.shape[0]
    rows = near_ref.shape[1] - 32
    row_index = lax.axis_index("row")
    parity = lax.rem(lax.axis_index("col"), 2)
    sums = jnp.zeros((8, 128), jnp.float32)
    for panel, pair in ((parity, (near_ref, far_ref)), (1 - parity, (near_mate_ref, far_mate_ref))):
        for place, source in enumerate(pair):
            for shard in range(half):
                at = snake_place(row_index ^ (masks[shard] + place), 2 * half, band)
                staged[panel, at] = source[shard, 0:rows, :]
                sums = sums + load_sums(source[shard, rows : rows + 16, :])
                sums = sums + load_sums(source[shard, rows + 16 : rows + 32, :])
    for shard in range(2 * half):
        for panel in range(2):
            top, lane = shard * rows, panel * PANEL
            keys[top : top + rows, lane : lane + PANEL] = staged[panel, shard]
    total = jnp.sum(jnp.sum(sums, axis=0, keepdims=True), axis=1, keepdims=True)
    amount = total * ridge_ref[0] / total_units
    amount_ref[...] = jnp.broadcast_to(amount, amount_ref.shape)
    held = keys[...]
    depth = held.shape[0]
    keys_ref[...] = held[:, PANEL:]
    gram = product(held[:, :PANEL], held, 0, 0)
    whole = jnp.concatenate([gram, held[:, :PANEL].astype(jnp.float32).T], axis=1)
    chunks = [whole[low : low + CHUNK] for low in range(0, PANEL, CHUNK)]
    solved, lower = eliminate_panel(chunks, [], ridge_of(amount), work)
    lower_ref[...] = lower
    for chunk, row in enumerate(solved):
        carried_ref[chunk] = row[:, PANEL:]
    middle = jnp.where(iota((depth, depth), 0) == iota((depth, depth), 1), 1.0, 0.0)
    middle_ref[...] = put_vectors(solved, middle, vectors_ref, heads_ref)


def second_kernel(
    amount_ref,
    carried_ref,
    middle_ref,
    keys_ref,
    lower_ref,
    vectors_ref,
    heads_ref,
    terms_ref,
    work,
):
    held = keys_ref[...]
    gram = product(held, held, 0, 0)
    whole = jnp.concatenate([gram, held.astype(jnp.float32).T], axis=1)
    chunks = [whole[low : low + CHUNK] for low in range(0, PANEL, CHUNK)]
    carried = [carried_ref[chunk] for chunk in range(PANEL // CHUNK)]
    solved, lower = eliminate_panel(chunks, carried, ridge_of(amount_ref[0:1, 0:1]), work)
    lower_ref[...] = lower
    middle = put_vectors(solved, middle_ref[...], vectors_ref, heads_ref)
    for place, term in enumerate(split_three(middle)):
        terms_ref[place] = term


def tile_kernel(
    sizes,
    amount_ref,
    terms_ref,
    heads_a_ref,
    heads_b_ref,
    vectors_a_ref,
    vectors_b_ref,
    lower_a_ref,
    lower_b_ref,
    rights_ref,
    *refs,
):
    band, col_units = sizes
    row_refs, refs = refs[:-11], refs[-11:]
    panel_a_ref, panel_b_ref, trailing_ref, forward_ref, *refs = refs
    blocks, right, out, staged, left, block_sems, out_sems = refs
    count, depth, width = blocks.shape
    row_units = left.shape[0]
    col_count = col_units // width
    row_index = lax.axis_index("row")
    col_index = lax.axis_index("col")
    in_a = row_index == 0
    in_b = row_index == band
    loads = [
        pltpu.make_async_copy(
            rights_ref.at[:, step * width : (step + 1) * width], blocks.at[step], block_sems.at[step]
        )
        for step in range(count)
    ]
    for load in loads:
        load.start()
    row_count, rows = staged.shape[0:2]
    part = lax.rem(row_index, band)
    for mask, source in enumerate(row_refs):
        for turn in range(band):
            row = (col_index ^ mask) * band + lax.rem(part - turn + band, band)
            staged[snake_place(row, row_count, band)] = source[turn]
    held = jnp.concatenate([staged[shard] for shard in range(row_count)], axis=0)
    flipped = held.astype(jnp.float32).T.astype(jnp.bfloat16)
    left[:, 0:depth] = flipped
    left[:, depth:] = flipped

    def put_right(step):
        if step < count:
            loads[step].wait()
            block = blocks[step]
            value = product(terms_ref[2], block, 1, 0) + product(terms_ref[1], block, 1, 0)
            value = value + product(terms_ref[0], block, 1, 0)
        else:
            first = (step - count) * width
            parts = (vectors_a_ref, vectors_b_ref)[first // PANEL : (first + width) // PANEL]
            value = jnp.concatenate([ref[...] for ref in parts], axis=1)
        high = value.astype(jnp.bfloat16)
        right[step % 2, 0:depth, :] = high
        right[step % 2, depth:, :] = (value - high.astype(jnp.float32)).astype(jnp.bfloat16)

    def copies(step):
        slot = step % SLOTS
        if step < count:
            target, at = trailing_ref, step * width
            if step >= col_count:
                target, at = forward_ref, (step - col_count) * width
            target = target.at[:, at : at + width]
            return [pltpu.make_async_copy(out.at[slot], target, out_sems.at[slot, 0])]
        first = (step - count) * width
        return [
            pltpu.make_async_copy(
                out.at[slot, :, lane : lane + PANEL],
                (panel_a_ref, panel_b_ref)[(first + lane) // PANEL],
                out_sems.at[slot, lane // PANEL],
            )
            for lane in range(0, width, PANEL)
        ]

    def finish_trailing(step, slot):
        apart = col_index * col_units + step * width - row_index * row_units

        amount = jnp.broadcast_to(amount_ref[0:1, 0:1], (64, 128))

        def add_ridge(piece, carry):
            top = pl.multiple_of(piece * 64, 64)
            lane = pl.multiple_of((top - apart) // 128 * 128, 128)
            near = iota((64, 128), 0) + (top - apart - lane) == iota((64, 128), 1)
            held = out[slot, pl.ds(top, 64), pl.ds(lane, 128)]
            out[slot, pl.ds(top, 64), pl.ds(lane, 128)] = held + jnp.where(near, amount, 0.0)
            return carry

        first = jnp.clip(apart, 0, row_units) // 64
        lax.fori_loop(first, jnp.clip(apart + width, 0, row_units) // 64, add_ridge, 0)

        @pl.when(in_a | in_b)
        def _():
            out[slot, 0:PANEL, :] = jnp.zeros((PANEL, width), jnp.float32)

        if step == 0:

            @pl.when(col_index < 2)
            def _():
                out[slot, :, 0:PANEL] = jnp.zeros((row_units, PANEL), jnp.float32)

    def finish_forward(step, slot):
        for here, heads in ((in_a, heads_a_ref), (in_b, heads_b_ref)):

            @pl.when(here)
            def _():
                block = blocks[step]
                out[slot, 0:PANEL, :] = product(heads[:, 0:depth], block, 1, 0) + product(
                    heads[:, depth:], block, 1, 0
                )

    def finish_panels(step, slot):
        for lane in range(0, width, PANEL):
            panel = ((step - count) * width + lane) // PANEL

            @pl.when(in_a)
            def _():
                block = jnp.zeros((PANEL, PANEL), jnp.float32)
                out[slot, 0:PANEL, lane : lane + PANEL] = block if panel else lower_a_ref[...]

            if panel:

                @pl.when(in_b)
                def _():
                    out[slot, 0:PANEL, lane : lane + PANEL] = lower_b_ref[...]

    steps = count + 2 * PANEL // width
    put_right(0)
    for step in range(steps):
        slot = step % SLOTS
        if step >= SLOTS:
            for copy in copies(step - SLOTS):
                copy.wait()
        if step + 1 < steps:
            put_right(step + 1)
        out[slot] = product(left[...], right[step % 2], 1, 0)
        if step < col_count:
            finish_trailing(step, slot)
        elif step < count:
            finish_forward(step, slot)
        else:
            finish_panels(step, slot)
        for copy in copies(step):
            copy.start()
    for step in range(steps - SLOTS, steps):
        for copy in copies(step):
            copy.wait()


def snake(row_count, band):
    lines = row_count // band
    order = [line * band for line in range(lines)]
    for line in reversed(range(lines)):
        places = [line * band + place for place in range(1, band)]
        order += places if (lines - 1 - line) % 2 == 0 else places[::-1]
    return order


def exchange(block, axis, count, step):
    return lax.ppermute(block, axis, [(place, place ^ step) for place in range(count)])


def on_device(edit_keys, edit_shifts, ridge_scale):
    row_count = lax.axis_size("row")
    col_count = lax.axis_size("col")
    rows, col_units = edit_keys.shape
    shift_cols = edit_shifts.shape[1]
    depth = rows * row_count
    total_units = col_units * col_count
    row_units = total_units // row_count
    band = row_count // col_count

    packed, shares, *pieces = pl.pallas_call(
        functools.partial(pack_kernel, band),
        out_shape=(
            jax.ShapeDtypeStruct((rows + 16, PANEL), jnp.bfloat16),
            jax.ShapeDtypeStruct((rows, col_units + shift_cols), jnp.bfloat16),
        )
        + (jax.ShapeDtypeStruct((rows, row_units), jnp.bfloat16),) * band,
        in_specs=[VMEM, VMEM],
        out_specs=(VMEM,) * (2 + band),
    )(edit_keys, edit_shifts)
    moved = []
    for turn in range(band):
        pairs = []
        for row in range(row_count):
            for col in range(col_count):
                target = (col * band + (row + turn) % band) * col_count + row // band
                pairs.append((row * col_count + col, target))
        moved.append(lax.ppermute(pieces[turn], ("row", "col"), pairs))
    near, sums = packed[:rows], packed[rows:]
    bit = col_count // 2
    while bit > 1:
        other = exchange(packed, "col", col_count, bit)
        low = (lax.axis_index("col") // bit) % 2 == 0
        near = jnp.where(low, packed[:rows], other[:rows])
        sums = [packed[rows:], other[rows:]]
        bit //= 2
        if bit > 1:
            sums = pl.pallas_call(
                add_kernel,
                out_shape=jax.ShapeDtypeStruct((16, PANEL), jnp.bfloat16),
                in_specs=[VMEM, VMEM],
                out_specs=VMEM,
            )(*sums)
            packed = jnp.concatenate([near, sums], axis=0)
    near = jnp.concatenate([near] + sums, axis=0)[None]
    order = snake(row_count, band)
    masks = [0]
    bit = row_count // 2
    while bit > 1:
        near = jnp.concatenate([near, exchange(near, "row", row_count, bit)], axis=0)
        masks += [held + bit for held in masks]
        if bit == row_count // 2:
            near, shares = lax.optimization_barrier((near, shares))
            rights = lax.all_gather(
                shares, "row", axis=0, tiled=True, axis_index_groups=[order]
            )
        bit //= 2
    far = exchange(near, "row", row_count, 1)
    near_mate = exchange(near, "col", col_count, 1)
    far_mate = exchange(far, "col", col_count, 1)

    part = functools.partial(jax.ShapeDtypeStruct, dtype=jnp.float32)
    part_low = functools.partial(jax.ShapeDtypeStruct, dtype=jnp.bfloat16)
    cost = pl.CostEstimate(flops=10**10, bytes_accessed=10**6, transcendentals=0)
    amount, lower_a, vectors_a, heads_a, carried, middle, keys_b = pl.pallas_call(
        functools.partial(first_kernel, total_units, masks, band),
        out_shape=(
            part((8, 128)),
            part((PANEL, PANEL)),
            part((depth, PANEL)),
            part_low((PANEL, 2 * depth)),
            part((PANEL // CHUNK, CHUNK, PANEL + depth)),
            part((depth, depth)),
            part_low((depth, PANEL)),
        ),
        in_specs=[SMEM] + [VMEM] * 4,
        out_specs=(VMEM,) * 7,
        scratch_shapes=[
            pltpu.VMEM((2, row_count, rows, PANEL), jnp.bfloat16),
            pltpu.VMEM((depth, 2 * PANEL), jnp.bfloat16),
            pltpu.VMEM((PANEL // CHUNK, CHUNK, CHUNK), jnp.float32),
        ],
        compiler_params=pltpu.CompilerParams(vmem_limit_bytes=32 * 2**20),
        cost_estimate=cost,
    )(ridge_scale, near, far, near_mate, far_mate)
    moved, amount = lax.optimization_barrier((moved, amount))
    row_keys = [jnp.stack(moved)]
    for mask in range(1, col_count):
        row_keys.append(exchange(row_keys[0], "col", col_count, mask))
    lower_b, vectors_b, heads_b, terms = pl.pallas_call(
        second_kernel,
        out_shape=(
            part((PANEL, PANEL)),
            part((depth, PANEL)),
            part_low((PANEL, 2 * depth)),
            part_low((3, depth, depth)),
        ),
        in_specs=[VMEM] * 4,
        out_specs=(VMEM,) * 4,
        scratch_shapes=[
            pltpu.VMEM((PANEL // CHUNK, CHUNK, CHUNK), jnp.float32),
        ],
        compiler_params=pltpu.CompilerParams(vmem_limit_bytes=32 * 2**20),
        cost_estimate=cost,
    )(amount, carried, middle, keys_b)

    width = 2 * PANEL
    if col_units % width or shift_cols % width:
        width = PANEL
    count = (col_units + shift_cols) // width
    return tuple(
        pl.pallas_call(
            functools.partial(tile_kernel, (band, col_units)),
            out_shape=(
                jax.ShapeDtypeStruct((row_units, PANEL), jnp.float32),
                jax.ShapeDtypeStruct((row_units, PANEL), jnp.float32),
                jax.ShapeDtypeStruct((row_units, col_units), jnp.float32),
                jax.ShapeDtypeStruct((row_units, shift_cols), jnp.float32),
            ),
            in_specs=[VMEM] * 8 + [ANY] + [VMEM] * col_count,
            out_specs=(ANY, ANY, ANY, ANY),
            scratch_shapes=[
                pltpu.VMEM((count, depth, width), jnp.bfloat16),
                pltpu.VMEM((2, 2 * depth, width), jnp.bfloat16),
                pltpu.VMEM((SLOTS, row_units, width), jnp.float32),
                pltpu.VMEM((row_count, rows, row_units), jnp.bfloat16),
                pltpu.VMEM((row_units, 2 * depth), jnp.bfloat16),
                pltpu.SemaphoreType.DMA((count,)),
                pltpu.SemaphoreType.DMA((SLOTS, 2)),
            ],
            compiler_params=pltpu.CompilerParams(vmem_limit_bytes=50 * 2**20),
            cost_estimate=pl.CostEstimate(
                flops=10**10, bytes_accessed=4 * 10**7, transcendentals=0
            ),
        )(
            amount,
            terms,
            heads_a,
            heads_b,
            vectors_a,
            vectors_b,
            lower_a,
            lower_b,
            rights,
            *row_keys,
        )
    )


def solution(mesh):
    return jax.shard_map(
        on_device,
        mesh=mesh,
        in_specs=(P("row", "col"), P("row", "col"), P()),
        out_specs=(P("row", None), P("row", None), P("row", "col"), P("row", "col")),
        check_vma=False,
    )
```

```python
import functools
import jax
import jax.numpy as jnp
from jax import lax
from jax.experimental import pallas as pl
from jax.experimental.pallas import tpu as pltpu
from jax.sharding import PartitionSpec as P

PANEL = 256
CHUNK = 128
GROUP = 32
SPAN = 16
SLOTS = 3
EXACT = lax.Precision.HIGHEST
VMEM = pl.BlockSpec(memory_space=pltpu.VMEM)
SMEM = pl.BlockSpec(memory_space=pltpu.SMEM)
ANY = pl.BlockSpec(memory_space=pl.ANY)


def iota(shape, dim):
    return lax.broadcasted_iota(jnp.int32, shape, dim)


def product(left_side, right_side, left_dim, right_dim, precision=None):
    return lax.dot_general(
        left_side,
        right_side,
        (((left_dim,), (right_dim,)), ((), ())),
        precision=precision,
        preferred_element_type=jnp.float32,
    )


def split_three(value):
    high = value.astype(jnp.bfloat16)
    rest = value - high.astype(jnp.float32)
    middle = rest.astype(jnp.bfloat16)
    low = (rest - middle.astype(jnp.float32)).astype(jnp.bfloat16)
    return high, middle, low


def store_sums(out_ref, top, sums):
    high, middle, low = (term.astype(jnp.float32) for term in split_three(sums))
    upper = jnp.concatenate([high, middle], axis=1)
    lower = jnp.concatenate([low, jnp.zeros_like(low)], axis=1)
    out_ref[top : top + 16, 0:256] = jnp.concatenate([upper, lower], axis=0).astype(jnp.bfloat16)


def load_sums(rows):
    wide = rows.astype(jnp.float32)
    return wide[0:8, 0:128] + wide[0:8, 128:256] + wide[8:16, 0:128]


def pack_kernel(keys_ref, packed_ref):
    rows, units = keys_ref.shape
    packed_ref[0:rows, :] = keys_ref[:, 0:PANEL]
    sums = jnp.zeros((8, 128), jnp.float32)
    for lane in range(0, units, 128):
        wide = keys_ref[:, lane : lane + 128].astype(jnp.float32)
        squares = wide * wide
        for top in range(0, rows, 8):
            sums = sums + squares[top : top + 8]
    store_sums(packed_ref, rows, sums)


def shares_kernel(band, keys_ref, shifts_ref, rights_ref, *piece_refs):
    units = keys_ref.shape[1]
    row_units = units // band
    rights_ref[:, 0:units] = keys_ref[...]
    rights_ref[:, units:] = shifts_ref[...]
    for turn in range(band):
        for part in range(band):

            @pl.when(lax.rem(lax.axis_index("row") + turn, band) == part)
            def _():
                piece_refs[turn][...] = keys_ref[:, part * row_units : (part + 1) * row_units]


def add_kernel(one_ref, other_ref, out_ref):
    store_sums(out_ref, 0, load_sums(one_ref[...]) + load_sums(other_ref[...]))


def factor_group(tiles, base):
    lane = iota((8, 128), 1)
    sub = iota((8, 128), 0)
    diagonals = []
    for start in range(0, len(tiles), SPAN // 8):
        columns = [
            {
                at: jnp.broadcast_to(tiles[at][:, lane_of : lane_of + 1], (8, 128))
                for at in range((lane_of - base) // 8, len(tiles))
            }
            for lane_of in range(base + 8 * start, base + 8 * start + SPAN)
        ]
        for q in range(SPAN):
            top, own = start + q // 8, q % 8
            first = base + 8 * start + q
            live = range(top, len(tiles))
            column = columns[q]
            pivot = jnp.broadcast_to(column[top][own : own + 1, :], (8, 128))
            inverse = 1.0 / pivot
            for k in range(q + 1, SPAN):
                near = start + k // 8
                factor = jnp.broadcast_to(column[near][k % 8 : k % 8 + 1, :], (8, 128)) * inverse
                for at in range(near, len(tiles)):
                    columns[k][at] = columns[k][at] - column[at] * factor
            row = jnp.broadcast_to(tiles[top][own : own + 1, :], (8, 128))
            row = jnp.where(lane == first, 1.0, row)
            scaled = row * inverse
            for at in live:
                kept = jnp.where(lane == first, 0.0, tiles[at])
                new = kept - column[at] * scaled
                if at == top:
                    new = jnp.where(sub < own, tiles[at], jnp.where(sub == own, row, new))
                tiles[at] = new
            if own == 0:
                scale = jnp.zeros((8, 128), jnp.float32)
                pivots = jnp.zeros((8, 128), jnp.float32)
            scale = jnp.where(sub == own, lax.rsqrt(pivot), scale)
            pivots = jnp.where(sub == own, pivot, pivots)
            if own == 7:
                tiles[top] = tiles[top] * scale
                diagonals.append(pivots * scale)
    return tiles, diagonals


def factor_chunk(work):
    lane = iota((CHUNK, CHUNK), 1)
    row = iota((CHUNK, CHUNK), 0)
    diagonals = []
    for base in range(0, CHUNK, GROUP):
        rest = base + GROUP
        tiles = [work[top : top + 8, :] for top in range(base, rest, 8)]
        tiles, found = factor_group(tiles, base)
        diagonals += found
        done = jnp.concatenate(tiles, axis=0)
        work[base:rest, :] = done
        if rest < CHUNK:
            group_lane = lane[base:rest]
            upper = (group_lane > row[base:rest]) & (group_lane < rest)
            update = product(done, jnp.where(upper, 0.0, done), 0, 0, EXACT)[rest:]
            later_lane = lane[rest:]
            own = (later_lane >= base) & (later_lane < rest)
            work[rest:, :] = jnp.where(own, 0.0, work[rest:, :]) - update
    both = work[...]
    diagonal = jnp.concatenate(diagonals, axis=0)
    inverse = jnp.where(lane <= row, both, 0.0)
    factor = jnp.where(lane > row, both, jnp.where(lane == row, diagonal, 0.0))
    return inverse, factor


def snake_place(row, row_count, band):
    lines = row_count // band
    line, place = row // band, lax.rem(row, band)
    back = lines - 1 - line
    inner = jnp.where(lax.rem(back, 2) == 0, place - 1, band - 1 - place)
    return jnp.where(place == 0, line, lines + back * (band - 1) + inner)


def eliminate_panel(rows, carried, ridge, work):
    solved = []
    factors = []
    for chunk, row in enumerate(rows):
        low, high = chunk * CHUNK, (chunk + 1) * CHUNK
        block = row[:, low:high] + ridge
        for done in carried + solved:
            block = block - product(done[:, low:high], done[:, low:high], 0, 0, EXACT)
        work[chunk] = block
        later = row[:, high:]
        for done in carried + solved:
            later = later - product(done[:, low:high], done[:, high:], 0, 0, EXACT)
        inverse, factor = factor_chunk(work.at[chunk])
        later = product(inverse, later, 1, 0, EXACT)
        solved.append(jnp.concatenate([jnp.zeros((CHUNK, high), jnp.float32), later], axis=1))
        factors.append(factor)
    square = jnp.zeros((CHUNK, CHUNK), jnp.float32)
    upper = jnp.concatenate([factors[0], solved[0][:, CHUNK : 2 * CHUNK]], axis=1)
    under = jnp.concatenate([square, factors[1]], axis=1)
    return solved, jnp.concatenate([upper, under], axis=0).T


def put_vectors(solved, middle, vectors_ref, heads_ref):
    depth = vectors_ref.shape[0]
    for chunk, row in enumerate(solved):
        low, high = chunk * CHUNK, (chunk + 1) * CHUNK
        vector = row[:, -depth:]
        vectors_ref[:, low:high] = vector.T
        first, second, _ = split_three(vector)
        heads_ref[low:high, 0:depth] = first
        heads_ref[low:high, depth : 2 * depth] = second
        middle = middle - product(vector, vector, 0, 0, EXACT)
    return middle


def ridge_of(amount):
    square = (CHUNK, CHUNK)
    near = iota(square, 0) == iota(square, 1)
    return jnp.where(near, jnp.broadcast_to(amount, square), 0.0)


def first_kernel(
    total_units,
    masks,
    band,
    ridge_ref,
    near_ref,
    far_ref,
    near_mate_ref,
    far_mate_ref,
    amount_ref,
    lower_ref,
    vectors_ref,
    heads_ref,
    carried_ref,
    middle_ref,
    keys_ref,
    staged,
    keys,
    work,
):
    half = near_ref.shape[0]
    rows = near_ref.shape[1] - 32
    row_index = lax.axis_index("row")
    parity = lax.rem(lax.axis_index("col"), 2)
    sums = jnp.zeros((8, 128), jnp.float32)
    for panel, pair in ((parity, (near_ref, far_ref)), (1 - parity, (near_mate_ref, far_mate_ref))):
        for place, source in enumerate(pair):
            for shard in range(half):
                at = snake_place(row_index ^ (masks[shard] + place), 2 * half, band)
                staged[panel, at] = source[shard, 0:rows, :]
                sums = sums + load_sums(source[shard, rows : rows + 16, :])
                sums = sums + load_sums(source[shard, rows + 16 : rows + 32, :])
    for shard in range(2 * half):
        for panel in range(2):
            top, lane = shard * rows, panel * PANEL
            keys[top : top + rows, lane : lane + PANEL] = staged[panel, shard]
    total = jnp.sum(jnp.sum(sums, axis=0, keepdims=True), axis=1, keepdims=True)
    amount = total * ridge_ref[0] / total_units
    amount_ref[...] = jnp.broadcast_to(amount, amount_ref.shape)
    held = keys[...]
    depth = held.shape[0]
    keys_ref[...] = held[:, PANEL:]
    gram = product(held[:, :PANEL], held, 0, 0)
    whole = jnp.concatenate([gram, held[:, :PANEL].astype(jnp.float32).T], axis=1)
    chunks = [whole[low : low + CHUNK] for low in range(0, PANEL, CHUNK)]
    solved, lower = eliminate_panel(chunks, [], ridge_of(amount), work)
    lower_ref[...] = lower
    for chunk, row in enumerate(solved):
        carried_ref[chunk] = row[:, PANEL:]
    middle = jnp.where(iota((depth, depth), 0) == iota((depth, depth), 1), 1.0, 0.0)
    middle_ref[...] = put_vectors(solved, middle, vectors_ref, heads_ref)


def second_kernel(
    amount_ref,
    carried_ref,
    middle_ref,
    keys_ref,
    lower_ref,
    vectors_ref,
    heads_ref,
    terms_ref,
    work,
):
    held = keys_ref[...]
    gram = product(held, held, 0, 0)
    whole = jnp.concatenate([gram, held.astype(jnp.float32).T], axis=1)
    chunks = [whole[low : low + CHUNK] for low in range(0, PANEL, CHUNK)]
    carried = [carried_ref[chunk] for chunk in range(PANEL // CHUNK)]
    solved, lower = eliminate_panel(chunks, carried, ridge_of(amount_ref[0:1, 0:1]), work)
    lower_ref[...] = lower
    middle = put_vectors(solved, middle_ref[...], vectors_ref, heads_ref)
    for place, term in enumerate(split_three(middle)):
        terms_ref[place] = term


def tile_kernel(
    sizes,
    amount_ref,
    terms_ref,
    heads_a_ref,
    heads_b_ref,
    vectors_a_ref,
    vectors_b_ref,
    lower_a_ref,
    lower_b_ref,
    rights_ref,
    *refs,
):
    band, col_units = sizes
    row_refs, refs = refs[:-11], refs[-11:]
    panel_a_ref, panel_b_ref, trailing_ref, forward_ref, *refs = refs
    blocks, right, out, staged, left, block_sems, out_sems = refs
    count, depth, width = blocks.shape
    row_units = left.shape[0]
    col_count = col_units // width
    row_index = lax.axis_index("row")
    col_index = lax.axis_index("col")
    in_a = row_index == 0
    in_b = row_index == band
    loads = [
        pltpu.make_async_copy(
            rights_ref.at[:, step * width : (step + 1) * width], blocks.at[step], block_sems.at[step]
        )
        for step in range(count)
    ]
    for load in loads:
        load.start()
    row_count, rows = staged.shape[0:2]
    part = lax.rem(row_index, band)
    for mask, source in enumerate(row_refs):
        for turn in range(band):
            row = (col_index ^ mask) * band + lax.rem(part - turn + band, band)
            staged[snake_place(row, row_count, band)] = source[turn]
    held = jnp.concatenate([staged[shard] for shard in range(row_count)], axis=0)
    flipped = held.astype(jnp.float32).T.astype(jnp.bfloat16)
    left[:, 0:depth] = flipped
    left[:, depth:] = flipped

    def put_right(step):
        if step < count:
            loads[step].wait()
            block = blocks[step]
            value = product(terms_ref[2], block, 1, 0) + product(terms_ref[1], block, 1, 0)
            value = value + product(terms_ref[0], block, 1, 0)
        else:
            first = (step - count) * width
            parts = (vectors_a_ref, vectors_b_ref)[first // PANEL : (first + width) // PANEL]
            value = jnp.concatenate([ref[...] for ref in parts], axis=1)
        high = value.astype(jnp.bfloat16)
        right[step % 2, 0:depth, :] = high
        right[step % 2, depth:, :] = (value - high.astype(jnp.float32)).astype(jnp.bfloat16)
        if step == 0:

            @pl.when(col_index < 2)
            def _():
                right[0, :, 0:PANEL] = jnp.zeros((2 * depth, PANEL), jnp.bfloat16)


    def copies(step):
        slot = step % SLOTS
        if step < count:
            target, at = trailing_ref, step * width
            if step >= col_count:
                target, at = forward_ref, (step - col_count) * width
            target = target.at[:, at : at + width]
            return [pltpu.make_async_copy(out.at[slot], target, out_sems.at[slot, 0])]
        first = (step - count) * width
        return [
            pltpu.make_async_copy(
                out.at[slot, :, lane : lane + PANEL],
                (panel_a_ref, panel_b_ref)[(first + lane) // PANEL],
                out_sems.at[slot, lane // PANEL],
            )
            for lane in range(0, width, PANEL)
        ]

    def finish_trailing(step, slot):
        apart = col_index * col_units + step * width - row_index * row_units

        amount = jnp.broadcast_to(amount_ref[0:1, 0:1], (64, 128))

        def add_ridge(piece, carry):
            top = pl.multiple_of(piece * 64, 64)
            lane = pl.multiple_of((top - apart) // 128 * 128, 128)
            near = iota((64, 128), 0) + (top - apart - lane) == iota((64, 128), 1)
            held = out[slot, pl.ds(top, 64), pl.ds(lane, 128)]
            out[slot, pl.ds(top, 64), pl.ds(lane, 128)] = held + jnp.where(near, amount, 0.0)
            return carry

        first = jnp.clip(apart, 0, row_units) // 64
        lax.fori_loop(first, jnp.clip(apart + width, 0, row_units) // 64, add_ridge, 0)

        @pl.when(in_a | in_b)
        def _():
            out[slot, 0:PANEL, :] = jnp.zeros((PANEL, width), jnp.float32)

    def finish_forward(step, slot):
        for here, heads in ((in_a, heads_a_ref), (in_b, heads_b_ref)):

            @pl.when(here)
            def _():
                block = blocks[step]
                out[slot, 0:PANEL, :] = product(heads[:, 0:depth], block, 1, 0) + product(
                    heads[:, depth:], block, 1, 0
                )

    def finish_panels(step, slot):
        for lane in range(0, width, PANEL):
            panel = ((step - count) * width + lane) // PANEL

            @pl.when(in_a)
            def _():
                block = jnp.zeros((PANEL, PANEL), jnp.float32)
                out[slot, 0:PANEL, lane : lane + PANEL] = block if panel else lower_a_ref[...]

            if panel:

                @pl.when(in_b)
                def _():
                    out[slot, 0:PANEL, lane : lane + PANEL] = lower_b_ref[...]

    steps = count + 2 * PANEL // width
    put_right(0)
    for step in range(steps):
        slot = step % SLOTS
        if step >= SLOTS:
            for copy in copies(step - SLOTS):
                copy.wait()
        if step + 1 < steps:
            put_right(step + 1)
        out[slot] = product(left[...], right[step % 2], 1, 0)
        if step < col_count:
            finish_trailing(step, slot)
        elif step < count:
            finish_forward(step, slot)
        else:
            finish_panels(step, slot)
        for copy in copies(step):
            copy.start()
    for step in range(steps - SLOTS, steps):
        for copy in copies(step):
            copy.wait()


def snake(row_count, band):
    lines = row_count // band
    order = [line * band for line in range(lines)]
    for line in reversed(range(lines)):
        places = [line * band + place for place in range(1, band)]
        order += places if (lines - 1 - line) % 2 == 0 else places[::-1]
    return order


def exchange(block, axis, count, step):
    return lax.ppermute(block, axis, [(place, place ^ step) for place in range(count)])


def on_device(edit_keys, edit_shifts, ridge_scale):
    row_count = lax.axis_size("row")
    col_count = lax.axis_size("col")
    rows, col_units = edit_keys.shape
    shift_cols = edit_shifts.shape[1]
    depth = rows * row_count
    total_units = col_units * col_count
    row_units = total_units // row_count
    band = row_count // col_count

    packed = pl.pallas_call(
        pack_kernel,
        out_shape=jax.ShapeDtypeStruct((rows + 16, PANEL), jnp.bfloat16),
        in_specs=[VMEM],
        out_specs=VMEM,
    )(edit_keys)
    shares, *pieces = pl.pallas_call(
        functools.partial(shares_kernel, band),
        out_shape=(jax.ShapeDtypeStruct((rows, col_units + shift_cols), jnp.bfloat16),)
        + (jax.ShapeDtypeStruct((rows, row_units), jnp.bfloat16),) * band,
        in_specs=[VMEM, VMEM],
        out_specs=(VMEM,) * (1 + band),
    )(edit_keys, edit_shifts)
    moved = []
    for turn in range(band):
        pairs = []
        for row in range(row_count):
            for col in range(col_count):
                target = (col * band + (row + turn) % band) * col_count + row // band
                pairs.append((row * col_count + col, target))
        moved.append(lax.ppermute(pieces[turn], ("row", "col"), pairs))
    near, sums = packed[:rows], packed[rows:]
    bit = col_count // 2
    while bit > 1:
        other = exchange(packed, "col", col_count, bit)
        low = (lax.axis_index("col") // bit) % 2 == 0
        near = jnp.where(low, packed[:rows], other[:rows])
        sums = [packed[rows:], other[rows:]]
        bit //= 2
        if bit > 1:
            sums = pl.pallas_call(
                add_kernel,
                out_shape=jax.ShapeDtypeStruct((16, PANEL), jnp.bfloat16),
                in_specs=[VMEM, VMEM],
                out_specs=VMEM,
            )(*sums)
            packed = jnp.concatenate([near, sums], axis=0)
    near = jnp.concatenate([near] + sums, axis=0)[None]
    order = snake(row_count, band)
    masks = [0]
    bit = row_count // 2
    while bit > 1:
        near = jnp.concatenate([near, exchange(near, "row", row_count, bit)], axis=0)
        masks += [held + bit for held in masks]
        if bit == row_count // 2:
            near, shares = lax.optimization_barrier((near, shares))
            rights = lax.all_gather(
                shares, "row", axis=0, tiled=True, axis_index_groups=[order]
            )
        bit //= 2
    far = exchange(near, "row", row_count, 1)
    near_mate = exchange(near, "col", col_count, 1)
    far_mate = exchange(far, "col", col_count, 1)

    part = functools.partial(jax.ShapeDtypeStruct, dtype=jnp.float32)
    part_low = functools.partial(jax.ShapeDtypeStruct, dtype=jnp.bfloat16)
    cost = pl.CostEstimate(flops=10**10, bytes_accessed=10**6, transcendentals=0)
    amount, lower_a, vectors_a, heads_a, carried, middle, keys_b = pl.pallas_call(
        functools.partial(first_kernel, total_units, masks, band),
        out_shape=(
            part((8, 128)),
            part((PANEL, PANEL)),
            part((depth, PANEL)),
            part_low((PANEL, 2 * depth)),
            part((PANEL // CHUNK, CHUNK, PANEL + depth)),
            part((depth, depth)),
            part_low((depth, PANEL)),
        ),
        in_specs=[SMEM] + [VMEM] * 4,
        out_specs=(VMEM,) * 7,
        scratch_shapes=[
            pltpu.VMEM((2, row_count, rows, PANEL), jnp.bfloat16),
            pltpu.VMEM((depth, 2 * PANEL), jnp.bfloat16),
            pltpu.VMEM((PANEL // CHUNK, CHUNK, CHUNK), jnp.float32),
        ],
        compiler_params=pltpu.CompilerParams(vmem_limit_bytes=32 * 2**20),
        cost_estimate=cost,
    )(ridge_scale, near, far, near_mate, far_mate)
    moved, amount = lax.optimization_barrier((moved, amount))
    row_keys = [jnp.stack(moved)]
    for mask in range(1, col_count):
        row_keys.append(exchange(row_keys[0], "col", col_count, mask))
    lower_b, vectors_b, heads_b, terms = pl.pallas_call(
        second_kernel,
        out_shape=(
            part((PANEL, PANEL)),
            part((depth, PANEL)),
            part_low((PANEL, 2 * depth)),
            part_low((3, depth, depth)),
        ),
        in_specs=[VMEM] * 4,
        out_specs=(VMEM,) * 4,
        scratch_shapes=[
            pltpu.VMEM((PANEL // CHUNK, CHUNK, CHUNK), jnp.float32),
        ],
        compiler_params=pltpu.CompilerParams(vmem_limit_bytes=32 * 2**20),
        cost_estimate=cost,
    )(amount, carried, middle, keys_b)

    width = 2 * PANEL
    if col_units % width or shift_cols % width:
        width = PANEL
    count = (col_units + shift_cols) // width
    return tuple(
        pl.pallas_call(
            functools.partial(tile_kernel, (band, col_units)),
            out_shape=(
                jax.ShapeDtypeStruct((row_units, PANEL), jnp.float32),
                jax.ShapeDtypeStruct((row_units, PANEL), jnp.float32),
                jax.ShapeDtypeStruct((row_units, col_units), jnp.float32),
                jax.ShapeDtypeStruct((row_units, shift_cols), jnp.float32),
            ),
            in_specs=[VMEM] * 8 + [ANY] + [VMEM] * col_count,
            out_specs=(ANY, ANY, ANY, ANY),
            scratch_shapes=[
                pltpu.VMEM((count, depth, width), jnp.bfloat16),
                pltpu.VMEM((2, 2 * depth, width), jnp.bfloat16),
                pltpu.VMEM((SLOTS, row_units, width), jnp.float32),
                pltpu.VMEM((row_count, rows, row_units), jnp.bfloat16),
                pltpu.VMEM((row_units, 2 * depth), jnp.bfloat16),
                pltpu.SemaphoreType.DMA((count,)),
                pltpu.SemaphoreType.DMA((SLOTS, 2)),
            ],
            compiler_params=pltpu.CompilerParams(vmem_limit_bytes=50 * 2**20),
            cost_estimate=pl.CostEstimate(
                flops=10**10, bytes_accessed=4 * 10**7, transcendentals=0
            ),
        )(
            amount,
            terms,
            heads_a,
            heads_b,
            vectors_a,
            vectors_b,
            lower_a,
            lower_b,
            rights,
            *row_keys,
        )
    )


def solution(mesh):
    return jax.shard_map(
        on_device,
        mesh=mesh,
        in_specs=(P("row", "col"), P("row", "col"), P()),
        out_specs=(P("row", None), P("row", None), P("row", "col"), P("row", "col")),
        check_vma=False,
    )
```
